128 devices in a mesh: group: 8 (over z, core), lane: 16 (over y, x).
Axes of the slice: x: 4, y: 4, z: 4, core: 2. Of those that a mesh axis runs over, the one named last changes fastest.
Arguments:
- tokens: bfloat16 [2048, 7168], P(('group', 'lane')), may hold values from -6 to 6
- expert_ids: int32 [2048, 8], P(('group', 'lane')), may hold values from 0 to 31, as said below
- gate_weights: float32 [2048, 8], P(('group', 'lane')), may hold values from 0.05 to 0.6
- w_gate: bfloat16 [128, 7168, 512], P(('group', 'lane')), may hold values from -0.0625 to 0.0625
- w_up: bfloat16 [128, 7168, 512], P(('group', 'lane')), may hold values from -0.0625 to 0.0625
- w_down: bfloat16 [128, 2048, 1792], P(('group', 'lane')), may hold values from -0.125 to 0.125
Outputs:
- moe_output: bfloat16 [2048, 7168], P(('group', 'lane'))
The draws below stay inside these ranges and needn't reach their ends.
Inputs may be any that keep to these rules, and one draw needn't show every extreme that they name: `expert_ids`: each row names 8 different experts that lie in at most 4 groups, expert e being in group e // 4. Among the 16 rows of one device no expert is named by more than 8 rows, and in every draw one expert is named by exactly 8 rows of every device.
All inputs are finite; a program needn't handle non-finite values.
Results may differ from the reference program's by a relative error of at most 0.012.
Values may be sent and summed in bfloat16 or wider, within the bound.
A program may use at most 128 MiB of HBM per device.

```python
import jax
import jax.numpy as jnp
from jax import lax

D = 7168
FF = 2048
TOPK = 8
GROUP_LIMIT = 4
HSPLIT = 4
TOK_DEV = 16
FF_DEV = 512
DCOL = 1792
EXP_GROUP = 4
EXPERTS = 32
TOKENS = 2048
CAP = 8
N_GROUP = 8


def draw_expert_ids(key, part):
    key = jax.random.fold_in(key, 7)
    key_pop, key_hot, key_block, key_row, key_group = jax.random.split(key, 5)
    block_count = TOKENS // TOK_DEV
    expert_range = jnp.arange(EXPERTS, dtype=jnp.int32)
    group_range = jnp.arange(N_GROUP, dtype=jnp.int32)
    membership = (expert_range[:, None] // EXP_GROUP == group_range[None, :]).astype(jnp.int32)
    popularity = jax.random.permutation(key_pop, EXPERTS).astype(jnp.int32)
    global_hot = jax.random.randint(key_hot, (), 0, EXPERTS)
    block_hot = jax.random.randint(key_block, (block_count,), 0, EXPERTS)
    row_noise = jax.random.randint(key_row, (block_count, TOK_DEV, EXPERTS), 0, 1024)
    group_noise = jax.random.randint(key_group, (block_count, TOK_DEV, N_GROUP), 0, 1024)

    def one_block(hot_expert, noise_rows, noise_groups):
        hot_mask = ((expert_range == global_hot) | (expert_range == hot_expert)).astype(jnp.int32)

        def one_row(counts, noises):
            expert_noise, group_part = noises
            free_flag = (counts < CAP).astype(jnp.int32)
            hot_flag = hot_mask * free_flag
            free_groups = jnp.sum(membership * free_flag[:, None], axis=0)
            hot_groups = jnp.sum(membership * hot_flag[:, None], axis=0)
            group_key = ((hot_groups * 32 + free_groups) * 1024 + group_part) * 64 + group_range
            top_groups = lax.top_k(group_key, GROUP_LIMIT)[1]
            group_flag = jnp.any(group_range[:, None] == top_groups[None, :], axis=1).astype(jnp.int32)
            allowed = jnp.sum(membership * group_flag[None, :], axis=1)
            expert_key = (((allowed * 2 + free_flag) * 2 + hot_flag) * 2048 + expert_noise + popularity * 16) * 64 + expert_range
            chosen = lax.top_k(expert_key, TOPK)[1].astype(jnp.int32)
            counts = counts + jnp.any(expert_range[:, None] == chosen[None, :], axis=1).astype(jnp.int32)
            return (counts, chosen)
        return lax.scan(one_row, jnp.zeros((EXPERTS,), jnp.int32), (noise_rows, noise_groups))[1]
    picked_all = jax.vmap(one_block)(block_hot, row_noise, group_noise)
    return picked_all.reshape(TOKENS, TOPK)


def block_levels(key, shape, cuts, smallest, high):
    gain, own = 1.0, jax.random.fold_in(key, 6)
    for position, shards_of in cuts:
        steps = jnp.exp(jax.random.uniform(jax.random.fold_in(own, position), (shards_of,), jnp.float32, smallest / len(cuts), high / len(cuts)))
        gain = gain * jnp.repeat(steps, shape[position] // shards_of).reshape([-1 if axis == position else 1 for axis in range(len(shape))])
    return gain


def centred(stream_key, shape, deviation, bound, pieces=(), held_as=jnp.bfloat16):
    result = deviation * jax.random.normal(stream_key, shape, jnp.float32)
    if pieces:
        result = result * block_levels(stream_key, shape, pieces, -0.22, 0.18)
    return jnp.clip(result, -bound, bound).astype(held_as)


def setup_inputs(seed: int = 0) -> dict:
    key_list = jax.random.split(jax.random.key(seed), 7)
    return {
        "tokens": centred(key_list[0], (TOKENS, D), 1.0, 6.0, ((0, 128),)),
        "expert_ids": draw_expert_ids(jax.random.fold_in(key_list[6], 71), 0),
        "gate_weights": jnp.clip(0.05 + 0.55 * jax.random.uniform(key_list[2], (TOKENS, TOPK), jnp.float32) ** block_levels(key_list[2], (TOKENS, TOPK), ((0, 128),), -0.2, 0.2), 0.05, 0.6),
        "w_gate": centred(key_list[3], (EXPERTS * HSPLIT, D, FF_DEV), D ** -0.5, 0.0625, ((0, 128),)),
        "w_up": centred(key_list[4], (EXPERTS * HSPLIT, D, FF_DEV), D ** -0.5, 0.0625, ((0, 128),)),
        "w_down": centred(key_list[5], (EXPERTS * HSPLIT, FF, DCOL), FF ** -0.5, 0.125, ((0, 128),)),
    }


def reference(tokens, expert_ids, gate_weights, w_gate, w_up, w_down):
    most_rows = (TOKENS // TOK_DEV) * CAP

    def expert_step(running, expert_index):
        chosen = expert_ids == expert_index
        weight = jnp.sum(jnp.where(chosen, gate_weights, 0.0), axis=1)
        named_rows = jnp.any(chosen, axis=1)
        row_index = jnp.nonzero(named_rows, size=most_rows, fill_value=0)[0].astype(jnp.int32)
        filled = jnp.arange(most_rows) < jnp.sum(named_rows.astype(jnp.int32))
        inputs = tokens[row_index]
        start = (expert_index * HSPLIT).astype(jnp.int32)
        gate_full = jnp.transpose(lax.dynamic_slice_in_dim(w_gate, start, HSPLIT, 0), (1, 0, 2)).reshape(D, FF)
        up_full = jnp.transpose(lax.dynamic_slice_in_dim(w_up, start, HSPLIT, 0), (1, 0, 2)).reshape(D, FF)
        down_full = jnp.transpose(lax.dynamic_slice_in_dim(w_down, start, HSPLIT, 0), (1, 0, 2)).reshape(FF, D)
        gate_values = jnp.dot(inputs, gate_full, preferred_element_type=jnp.float32)
        up_values = jnp.dot(inputs, up_full, preferred_element_type=jnp.float32)
        hidden = (jax.nn.silu(gate_values) * up_values).astype(jnp.bfloat16)
        expert_out = jnp.dot(hidden, down_full, preferred_element_type=jnp.float32).astype(jnp.bfloat16)
        scaled = expert_out.astype(jnp.float32) * jnp.where(filled, weight[row_index], 0.0)[:, None]
        return running.at[row_index].add(scaled), None

    running = jnp.zeros((TOKENS, D), jnp.float32)
    running = lax.scan(expert_step, running, jnp.arange(EXPERTS, dtype=jnp.int32))[0]
    return running.astype(jnp.bfloat16)
```

```python
import jax
import jax.numpy as jnp
from jax import lax
from jax.experimental import pallas as pl
from jax.experimental.pallas import tpu as pltpu
from jax.sharding import PartitionSpec as P

TOPK = 8
CAP = 8
RING = 4
TOK = 16
META = 128
MESH = pl.DeviceIdType.MESH
BF16 = jnp.bfloat16
F32 = jnp.float32
STEPS = (0, 1, 3, 2)
LAG = 2


def iota(shape, dim):
    return lax.broadcasted_iota(jnp.int32, shape, dim)


def routing_rows(ids, gates):
    lane = iota((TOK, META), 1)
    picked = jnp.zeros((TOK, META), F32)
    high = jnp.zeros((TOK, META), F32)
    low = jnp.zeros((TOK, META), F32)
    for k in range(TOPK):
        name = ids[:, k : k + 1]
        gate = gates[:, k : k + 1]
        picked = jnp.where(lane == name, 1.0, picked)
        high = jnp.where(lane == name + 32, gate, high)
        low = jnp.where(lane == name + 64, gate, low)
    earlier = jnp.where(iota((TOK, TOK), 1) < iota((TOK, TOK), 0), 1.0, 0.0)
    before = jnp.dot(earlier, picked, preferred_element_type=F32)
    slot = jnp.where(picked > 0.5, before, -1.0)
    low = low - low.astype(BF16).astype(F32)
    return jnp.where(lane < 32, slot, jnp.where(lane < 64, high, low)).astype(BF16)


def kernel(
    tok_hbm, ids_ref, gates_ref, wg_hbm, wu_hbm, wd_hbm, out_ref,
    wg, wu, wd, blocks, chooser, own_rows, sib_out, sib_in, meta_in, hid, mix_own, mix_sib,
    part, part_out, part_in, q, a_in, r, b_in, t, x_in,
    load_sem, blk_send, blk_recv, sel_send, sel_recv, met_send, met_recv, hid_send, hid_recv,
    prt_send, prt_recv, a_send, a_recv, b_send, b_recv, x_send, x_recv,
):
    width = wg.shape[0]
    ff = wg.shape[1]
    cols = wd.shape[1]
    group, lane_index = lax.axis_index("group"), lax.axis_index("lane")
    z, c = group // 2, lax.rem(group, 2)
    y, x = lane_index // RING, lax.rem(lane_index, RING)
    a = (1 - c) * y + c * z
    b = (1 - c) * z + c * y

    def plus(v, d):
        return lax.rem(v + d, RING)

    def device(da, dx, db):
        a2, b2 = plus(a, da), plus(b, db)
        return (((1 - c) * b2 + c * a2) * 2 + c, ((1 - c) * a2 + c * b2) * RING + plus(x, dx))

    def place(da, dx, db):
        return plus(b, db) * (RING * RING) + plus(a, da) * RING + plus(x, dx)

    sibling = (z * 2 + 1 - c, lane_index)
    own_expert = group * RING + y
    sib_expert = (z * 2 + 1 - c) * RING + y

    def remote(src, dst, send, recv, target):
        return pltpu.make_async_remote_copy(
            src_ref=src, dst_ref=dst, send_sem=send, recv_sem=recv, device_id=target, device_id_type=MESH
        )

    mine = place(0, 0, 0)
    loads = [
        pltpu.make_async_copy(tok_hbm, blocks.at[mine, :, pl.ds(0, width)], load_sem.at[0]),
        pltpu.make_async_copy(wg_hbm.at[0], wg, load_sem.at[1]),
        pltpu.make_async_copy(wu_hbm.at[0], wu, load_sem.at[2]),
        pltpu.make_async_copy(wd_hbm.at[0], wd, load_sem.at[3]),
    ]
    for load in loads:
        load.start()

    peers = [sibling]
    for d in (1, 3, 2):
        peers += [device(d, 0, 0), device(0, d, 0), device(0, 0, d)]
    barrier = pltpu.get_barrier_semaphore()
    for peer in peers:
        pl.semaphore_signal(barrier, inc=1, device_id=peer, device_id_type=MESH)

    blocks[mine, :, pl.ds(width, META)] = routing_rows(ids_ref[...], gates_ref[...])
    loads[0].wait()
    pl.semaphore_wait(barrier, len(peers))

    sent = [0]

    def send_block(s, target):
        remote(blocks.at[s], blocks.at[s], blk_send.at[sent[0]], blk_recv.at[s], target).start()
        sent[0] += 1

    def wait_block(s):
        remote(blocks.at[s], blocks.at[s], blk_send.at[0], blk_recv.at[s], sibling).wait_recv()

    order = [(dx, da) for dx in STEPS for da in STEPS]

    def forward(k):
        dx, da = order[k]
        came, goes = (3, 1) if k % 2 == 0 else (1, 3)
        s = place(da, dx, came)
        wait_block(s)
        send_block(s, device(0, 0, goes))

    for d in (1, 3, 2):
        send_block(mine, device(d, 0, 0))
    for k, (dx, da) in enumerate(order):
        s = place(da, dx, 0)
        if k > 0:
            wait_block(s)
        if dx == 0:
            for d in (1, 3, 2):
                send_block(s, device(0, d, 0))
        send_block(s, device(0, 0, 1))
        send_block(s, device(0, 0, 3))
        if k >= LAG:
            forward(k - LAG)

    def base(i):
        return plus(b, STEPS[i]) * (RING * RING)

    def select_send(i):
        return remote(sib_out, sib_in.at[i % 2], sel_send.at[i], sel_recv.at[i], sibling)

    def meta_send(i):
        return remote(
            blocks.at[pl.ds(base(i), 16), :, pl.ds(width, META)], meta_in.at[i], met_send.at[i], met_recv.at[i], sibling
        )

    def select(i):
        meta = blocks[pl.ds(base(i), 16), :, pl.ds(width, META)].reshape(256, META)
        row, lane = iota((16, META), 0), iota((16, META), 1)
        want = jnp.where(row == 0, own_expert, sib_expert)
        pick = jnp.where(lane == want, 1.0, 0.0).astype(BF16)
        slots = lax.dot_general(pick, meta, (((1,), (1,)), ((), ())), preferred_element_type=F32)
        row, col = iota((256, 256), 0), iota((256, 256), 1)
        slot = jnp.where(row < 128, slots[0:1, :], slots[1:2, :])
        same = ((row & 127) >> 3) == (col >> 4)
        taken = slot == (row & 7).astype(F32)
        chooser[...] = jnp.where(same & taken, 1.0, 0.0).astype(BF16)
        if i > 0:
            select_send(i - 1).wait_send()

        def step(j, carry):
            at = pl.ds(pl.multiple_of(j * 1024, 1024), 1024)
            rows = blocks[pl.ds(base(i), 16), :, at].reshape(256, 1024)
            got = jnp.dot(chooser[...], rows, preferred_element_type=F32).astype(BF16)
            own_rows[:, at] = got[:128]
            sib_out[:, at] = got[128:]
            return carry

        lax.fori_loop(0, width // 1024, step, 0)
        select_send(i).start()
        meta_send(i).start()

    def hid_copy(i, d):
        return remote(hid.at[i, x], hid.at[i, x], hid_send.at[i * 3 + d - 1], hid_recv.at[i * RING + x], device(0, d, 0))

    def gate_up(i):
        select_send(i).wait_recv()

        def step(n, carry):
            at = pl.ds(pl.multiple_of(n * 256, 256), 256)
            rows = jnp.concatenate([own_rows[...], sib_in[i % 2]], axis=0)
            gate = jnp.dot(rows, wg[:, at], preferred_element_type=F32)
            up = jnp.dot(rows, wu[:, at], preferred_element_type=F32)
            hid[i, x, :, at] = (gate / (1.0 + jnp.exp(-gate)) * up).astype(BF16)
            return carry

        lax.fori_loop(0, ff // 256, step, 0)
        for d in (1, 3, 2):
            hid_copy(i, d).start()

    def mixer(meta):
        lane = iota((256, META), 1)
        meta = meta.astype(F32)

        def column(at):
            return jnp.sum(jnp.where(lane == at, meta, 0.0), axis=1, keepdims=True)

        slot, high, low = column(own_expert), column(own_expert + 32), column(own_expert + 64)
        row, col = iota((256, 256), 0), iota((256, 256), 1)
        same = (row >> 4) == ((col & 127) >> 3)
        taken = slot == (col & 7).astype(F32)
        return jnp.where(same & taken, jnp.where(col < 128, high, low), 0.0).astype(BF16)

    def part_send(i):
        return remote(part_out, part_in.at[i % 2], prt_send.at[i], prt_recv.at[i], sibling)

    def finish(i):
        meta_send(i).wait_recv()
        mix_own[...] = mixer(blocks[pl.ds(base(i), 16), :, pl.ds(width, META)].reshape(256, META))
        mix_sib[...] = mixer(meta_in[i].reshape(256, META))
        for d in (1, 3, 2):
            s = plus(x, d)
            remote(hid.at[i, s], hid.at[i, s], hid_send.at[0], hid_recv.at[i * RING + s], sibling).wait_recv()
        if i > 0:
            part_send(i - 1).wait_send()

        def step(j, carry):
            at = pl.ds(pl.multiple_of(j * 256, 256), 256)
            total = jnp.zeros((256, 256), F32)
            for s in range(RING):
                total += jnp.dot(hid[i, s], wd[pl.ds(s * ff, ff), at], preferred_element_type=F32)
            total = total.astype(BF16)
            for_own = jnp.concatenate([total[:128], total[:128]], axis=0)
            for_sib = jnp.concatenate([total[128:], total[128:]], axis=0)
            part[:, at] = jnp.dot(mix_own[...], for_own, preferred_element_type=F32)
            part_out[:, at] = jnp.dot(mix_sib[...], for_sib, preferred_element_type=F32).astype(BF16)
            return carry

        lax.fori_loop(0, cols // 256, step, 0)
        part_send(i).start()

    def piece(v):
        return pl.ds(pl.multiple_of(v * 64, 64), 64)

    def a_copy(i, d):
        return remote(
            q.at[i % 2, piece(plus(a, d))], a_in.at[i, d - 1], a_send.at[i * 3 + d - 1], a_recv.at[i * 3 + d - 1], device(d, 0, 0)
        )

    def join(i):
        part_send(i).wait_recv()
        if i >= 2:
            for d in (1, 3, 2):
                a_copy(i - 2, d).wait_send()

        def step(j, carry):
            at = pl.ds(pl.multiple_of(j * 64, 64), 64)
            q[i % 2, at, :] = (part[at, :] + part_in[i % 2, at, :].astype(F32)).astype(BF16)
            return carry

        lax.fori_loop(0, RING, step, 0)
        for d in (2, 1, 3):
            a_copy(i, d).start()

    def b_copy(i):
        return remote(r.at[i], b_in.at[i - 1], b_send.at[i - 1], b_recv.at[i - 1], device(0, 0, STEPS[i]))

    def reduce_a(i):
        for d in (1, 3, 2):
            a_copy(i, d).wait_recv()
        total = q[i % 2, piece(a), :].astype(F32)
        for d in range(3):
            total += a_in[i, d].astype(F32)
        r[i] = total.astype(BF16)
        if i > 0:
            b_copy(i).start()

    def wait_chunk(i):
        for k, (dx, da) in enumerate(order):
            waited = (STEPS[i] == 3 and k % 2 == 0) or (STEPS[i] == 1 and k % 2 == 1)
            if not waited:
                wait_block(place(da, dx, STEPS[i]))

    select(0)
    for k in range(len(order) - LAG, len(order)):
        forward(k)
    loads[1].wait()
    loads[2].wait()
    gate_up(0)
    loads[3].wait()
    wait_chunk(1)
    select(1)
    finish(0)
    gate_up(1)
    join(0)
    wait_chunk(2)
    select(2)
    finish(1)
    gate_up(2)
    join(1)
    reduce_a(0)
    wait_chunk(3)
    select(3)
    finish(2)
    gate_up(3)
    join(2)
    reduce_a(1)
    finish(3)
    join(3)
    reduce_a(2)
    reduce_a(3)

    total = r[0].astype(F32)
    for i in (1, 2, 3):
        b_copy(i).wait_recv()
        total += b_in[i - 1].astype(F32)
    t[...] = total.astype(BF16)

    def x_copy(d):
        rows = pl.ds(pl.multiple_of(plus(x, d) * TOK, TOK), TOK)
        return remote(t.at[rows], x_in.at[d - 1], x_send.at[d - 1], x_recv.at[d - 1], device(0, d, 0))

    def out_cols(v):
        return pl.ds(pl.multiple_of(v * cols, 128), cols)

    for d in (2, 1, 3):
        x_copy(d).start()
    out_ref[:, out_cols(x)] = t[pl.ds(pl.multiple_of(x * TOK, TOK), TOK), :]
    for d in (1, 3, 2):
        x_copy(d).wait_recv()
        out_ref[:, out_cols(plus(x, RING - d))] = x_in[d - 1]

    for n in range(sent[0]):
        remote(blocks.at[0], blocks.at[0], blk_send.at[n], blk_recv.at[0], sibling).wait_send()
    select_send(3).wait_send()
    part_send(3).wait_send()
    for i in range(4):
        meta_send(i).wait_send()
        for d in (1, 3, 2):
            hid_copy(i, d).wait_send()
            if i >= 2:
                a_copy(i, d).wait_send()
        if i > 0:
            b_copy(i).wait_send()
            x_copy(i).wait_send()


def per_device(tokens, expert_ids, gate_weights, w_gate, w_up, w_down):
    rows, width = tokens.shape
    ff = w_gate.shape[2]
    cols = w_down.shape[2]
    dma = pltpu.SemaphoreType.DMA
    vmem = pltpu.VMEM
    return pl.pallas_call(
        kernel,
        out_shape=jax.ShapeDtypeStruct((rows, width), BF16),
        in_specs=[
            pl.BlockSpec(memory_space=pl.ANY),
            pl.BlockSpec(memory_space=pltpu.VMEM),
            pl.BlockSpec(memory_space=pltpu.VMEM),
            pl.BlockSpec(memory_space=pl.ANY),
            pl.BlockSpec(memory_space=pl.ANY),
            pl.BlockSpec(memory_space=pl.ANY),
        ],
        out_specs=pl.BlockSpec(memory_space=pltpu.VMEM),
        scratch_shapes=[
            vmem((width, ff), BF16),
            vmem((width, ff), BF16),
            vmem((RING * ff, cols), BF16),
            vmem((64, TOK, width + META), BF16),
            vmem((256, 256), BF16),
            vmem((128, width), BF16),
            vmem((128, width), BF16),
            vmem((2, 128, width), BF16),
            vmem((4, 16, TOK, META), BF16),
            vmem((4, RING, 256, ff), BF16),
            vmem((256, 256), BF16),
            vmem((256, 256), BF16),
            vmem((256, cols), F32),
            vmem((256, cols), BF16),
            vmem((2, 256, cols), BF16),
            vmem((2, 256, cols), BF16),
            vmem((4, 3, 64, cols), BF16),
            vmem((4, 64, cols), BF16),
            vmem((3, 64, cols), BF16),
            vmem((64, cols), BF16),
            vmem((3, TOK, cols), BF16),
            dma((4,)),
            dma((64,)),
            dma((64,)),
            dma((4,)),
            dma((4,)),
            dma((4,)),
            dma((4,)),
            dma((12,)),
            dma((16,)),
            dma((4,)),
            dma((4,)),
            dma((12,)),
            dma((12,)),
            dma((3,)),
            dma((3,)),
            dma((3,)),
            dma((3,)),
        ],
        compiler_params=pltpu.CompilerParams(
            collective_id=0, has_side_effects=True, vmem_limit_bytes=62 * 2**20
        ),
        cost_estimate=pl.CostEstimate(flops=24 * 10**9, bytes_accessed=24 * 10**6, transcendentals=10**6),
    )(tokens, expert_ids, gate_weights, w_gate, w_up, w_down)


def solution(mesh):
    in_specs = (
        P(("group", "lane"), None),
        P(("group", "lane"), None),
        P(("group", "lane"), None),
        P(("group", "lane"), None, None),
        P(("group", "lane"), None, None),
        P(("group", "lane"), None, None),
    )
    out_specs = P(("group", "lane"), None)
    return jax.shard_map(
        per_device, mesh=mesh, in_specs=in_specs, out_specs=out_specs, check_vma=False
    )
```

```python
import jax
import jax.numpy as jnp
from jax import lax
from jax.experimental import pallas as pl
from jax.experimental.pallas import tpu as pltpu
from jax.sharding import PartitionSpec as P

TOPK = 8
CAP = 8
RING = 4
TOK = 16
META = 128
MESH = pl.DeviceIdType.MESH
BF16 = jnp.bfloat16
F32 = jnp.float32
STEPS = (0, 1, 3, 2)


def iota(shape, dim):
    return lax.broadcasted_iota(jnp.int32, shape, dim)


def routing_rows(ids, gates):
    unit = jnp.where(iota((TOPK, TOPK), 0) == iota((TOPK, TOPK), 1), 1.0, 0.0).astype(BF16)

    def turned(values):
        return lax.dot_general(values.astype(BF16), unit, (((0,), (0,)), ((), ())), preferred_element_type=F32)

    ids = turned(ids.astype(F32)).astype(jnp.int32)
    upper = gates.astype(BF16).astype(F32)
    lower = turned(gates - upper)
    upper = turned(upper)
    lane = iota((TOK, META), 1)
    picked = jnp.zeros((TOK, META), F32)
    high = jnp.zeros((TOK, META), F32)
    low = jnp.zeros((TOK, META), F32)
    for k in range(TOPK):
        name = ids[:, k : k + 1]
        picked = jnp.where(lane == name, 1.0, picked)
        high = jnp.where(lane == name + 32, upper[:, k : k + 1], high)
        low = jnp.where(lane == name + 64, lower[:, k : k + 1], low)
    earlier = jnp.where(iota((TOK, TOK), 1) < iota((TOK, TOK), 0), 1.0, 0.0)
    before = jnp.dot(earlier, picked, preferred_element_type=F32)
    slot = jnp.where(picked > 0.5, before, -1.0)
    return jnp.where(lane < 32, slot, jnp.where(lane < 64, high, low)).astype(BF16)


def kernel(
    tok_hbm, ids_ref, gates_ref, wg_hbm, wu_hbm, wd_hbm, out_ref,
    wg, wu, wd, blocks, chooser, rows, sib_out, meta_in, hid, mix_own, mix_sib,
    part, part_out, part_in, q, b_in, r, a_in, last, x_in,
    load_sem, blk_send, blk_recv, sel_send, sel_recv, met_send, met_recv, hid_send, hid_recv,
    prt_send, prt_recv, b_send, b_recv, a_send, a_recv, x_send, x_recv,
):
    width = wg.shape[0]
    ff = wg.shape[1]
    cols = wd.shape[1]
    group, lane_index = lax.axis_index("group"), lax.axis_index("lane")
    z, c = group // 2, lax.rem(group, 2)
    y, x = lane_index // RING, lax.rem(lane_index, RING)
    a = (1 - c) * y + c * z
    b = (1 - c) * z + c * y

    def plus(v, d):
        return lax.rem(v + d, RING)

    def device(da, dx, db):
        a2, b2 = plus(a, da), plus(b, db)
        return (((1 - c) * b2 + c * a2) * 2 + c, ((1 - c) * a2 + c * b2) * RING + plus(x, dx))

    def place(da, dx, db):
        return plus(a, da) * (RING * RING) + plus(b, db) * RING + plus(x, dx)

    sibling = (z * 2 + 1 - c, lane_index)
    own_expert = group * RING + y
    sib_expert = (z * 2 + 1 - c) * RING + y

    def remote(src, dst, send, recv, target):
        return pltpu.make_async_remote_copy(
            src_ref=src, dst_ref=dst, send_sem=send, recv_sem=recv, device_id=target, device_id_type=MESH
        )

    mine = place(0, 0, 0)
    loads = [
        pltpu.make_async_copy(tok_hbm, blocks.at[mine, :, pl.ds(0, width)], load_sem.at[0]),
        pltpu.make_async_copy(wg_hbm.at[0], wg, load_sem.at[1]),
        pltpu.make_async_copy(wu_hbm.at[0], wu, load_sem.at[2]),
        pltpu.make_async_copy(wd_hbm.at[0], wd, load_sem.at[3]),
    ]
    for load in loads:
        load.start()

    peers = [sibling]
    for d in (1, 3, 2):
        peers += [device(d, 0, 0), device(0, d, 0), device(0, 0, d)]
    barrier = pltpu.get_barrier_semaphore()
    for peer in peers:
        pl.semaphore_signal(barrier, inc=1, device_id=peer, device_id_type=MESH)

    blocks[mine, :, pl.ds(width, META)] = routing_rows(ids_ref[...], gates_ref[...])
    loads[0].wait()
    pl.semaphore_wait(barrier, len(peers))

    sent = [0]
    order = [(da, dx) for da in STEPS for dx in STEPS]

    def send_block(s, target):
        remote(blocks.at[s], blocks.at[s], blk_send.at[sent[0]], blk_recv.at[s], target).start()
        sent[0] += 1

    def wait_block(s):
        remote(blocks.at[s], blocks.at[s], blk_send.at[0], blk_recv.at[s], sibling).wait_recv()

    def along_x(i):
        s = place(STEPS[i], 0, 0)
        if i > 0:
            wait_block(s)
        send_block(s, device(0, 1, 0))
        send_block(s, device(0, 3, 0))

    def own(k):
        da, dx = order[k]
        s = place(da, dx, 0)
        if dx != 0:
            wait_block(s)
        if dx == (3, 1)[k // RING % 2]:
            send_block(s, device(0, RING - dx, 0))
        send_block(s, device(0, 0, 1))
        send_block(s, device(0, 0, 3))

    def forward(k):
        da, dx = order[k]
        came, goes = (3, 1) if k % 2 == 0 else (1, 3)
        s = place(da, dx, came)
        wait_block(s)
        send_block(s, device(0, 0, goes))

    def wait_chunk(i):
        for k in range(i * RING, i * RING + RING):
            da, dx = order[k]
            for db in (1, 3, 2):
                if db != (3, 1)[k % 2]:
                    wait_block(place(da, dx, db))

    def base(i):
        return plus(a, STEPS[i]) * (RING * RING)

    def select_send(i):
        return remote(sib_out, rows.at[i % 2, pl.ds(128, 128)], sel_send.at[i], sel_recv.at[i], sibling)

    def meta_send(i):
        return remote(
            blocks.at[pl.ds(base(i), 16), :, pl.ds(width, META)], meta_in.at[i], met_send.at[i], met_recv.at[i], sibling
        )

    def select(i):
        meta = blocks[pl.ds(base(i), 16), :, pl.ds(width, META)].reshape(256, META)
        row, lane = iota((16, META), 0), iota((16, META), 1)
        want = jnp.where(row == 0, own_expert, sib_expert)
        pick = jnp.where(lane == want, 1.0, 0.0).astype(BF16)
        slots = lax.dot_general(pick, meta, (((1,), (1,)), ((), ())), preferred_element_type=F32)
        row, col = iota((256, 256), 0), iota((256, 256), 1)
        slot = jnp.where(row < 128, slots[0:1, :], slots[1:2, :])
        same = ((row & 127) >> 3) == (col >> 4)
        taken = slot == (row & 7).astype(F32)
        chooser[...] = jnp.where(same & taken, 1.0, 0.0).astype(BF16)
        if i > 0:
            select_send(i - 1).wait_send()

        def step(j, carry):
            at = pl.ds(pl.multiple_of(j * 1024, 1024), 1024)
            tokens = blocks[pl.ds(base(i), 16), :, at].reshape(256, 1024)
            got = jnp.dot(chooser[...], tokens, preferred_element_type=F32).astype(BF16)
            rows[i % 2, pl.ds(0, 128), at] = got[:128]
            sib_out[:, at] = got[128:]
            return carry

        lax.fori_loop(0, width // 1024, step, 0)
        select_send(i).start()
        meta_send(i).start()

    def hid_copy(i, owner, h, target, n):
        at = hid.at[i, owner, pl.ds(h * 128, 128)]
        return remote(at, at, hid_send.at[i * 6 + n], hid_recv.at[(i * RING + owner) * 2 + h], device(0, target, 0))

    def gate_up(i):
        select_send(i).wait_recv()

        def step(n, carry):
            at = pl.ds(pl.multiple_of(n * 256, 256), 256)
            gate = jnp.dot(rows[i % 2], wg[:, at], preferred_element_type=F32)
            up = jnp.dot(rows[i % 2], wu[:, at], preferred_element_type=F32)
            hid[i, x, :, at] = (gate / (1.0 + jnp.exp(-gate)) * up).astype(BF16)
            return carry

        lax.fori_loop(0, ff // 256, step, 0)
        hid_copy(i, x, 0, 1, 0).start()
        hid_copy(i, x, 1, 3, 1).start()
        hid_copy(i, x, 1, 1, 2).start()
        hid_copy(i, x, 0, 3, 3).start()

    def hid_forward(i):
        hid_copy(i, plus(x, 3), 0, 1, 4).wait_recv()
        hid_copy(i, plus(x, 3), 0, 1, 4).start()
        hid_copy(i, plus(x, 1), 1, 3, 5).wait_recv()
        hid_copy(i, plus(x, 1), 1, 3, 5).start()

    def mixer(meta):
        lane = iota((256, META), 1)
        meta = meta.astype(F32)

        def column(at):
            return jnp.sum(jnp.where(lane == at, meta, 0.0), axis=1, keepdims=True)

        slot, high, low = column(own_expert), column(own_expert + 32), column(own_expert + 64)
        row, col = iota((256, 256), 0), iota((256, 256), 1)
        same = (row >> 4) == ((col & 127) >> 3)
        taken = slot == (col & 7).astype(F32)
        return jnp.where(same & taken, jnp.where(col < 128, high, low), 0.0).astype(BF16)

    def part_send(i):
        return remote(part_out, part_in.at[i % 2], prt_send.at[i], prt_recv.at[i], sibling)

    def finish(i):
        meta_send(i).wait_recv()
        mix_own[...] = mixer(blocks[pl.ds(base(i), 16), :, pl.ds(width, META)].reshape(256, META))
        mix_sib[...] = mixer(meta_in[i].reshape(256, META))
        hid_copy(i, plus(x, 3), 1, 1, 0).wait_recv()
        hid_copy(i, plus(x, 1), 0, 1, 0).wait_recv()
        hid_copy(i, plus(x, 2), 0, 1, 0).wait_recv()
        hid_copy(i, plus(x, 2), 1, 1, 0).wait_recv()
        if i > 0:
            part_send(i - 1).wait_send()

        def step(j, carry):
            at = pl.ds(pl.multiple_of(j * 896, 896), 896)
            hidden = jnp.concatenate([hid[i, s] for s in range(RING)], axis=1)
            total = jnp.dot(hidden, wd[:, at], preferred_element_type=F32).astype(BF16)
            for_own = jnp.concatenate([total[:128], total[:128]], axis=0)
            for_sib = jnp.concatenate([total[128:], total[128:]], axis=0)
            part_out[:, at] = jnp.dot(mix_sib[...], for_sib, preferred_element_type=F32).astype(BF16)
            part[:, at] = jnp.dot(mix_own[...], for_own, preferred_element_type=F32).astype(BF16)
            return carry

        lax.fori_loop(0, cols // 896, step, 0)
        part_send(i).start()

    def b_copy(i, d):
        at = pl.ds(pl.multiple_of(plus(b, d) * 64, 64), 64)
        n = i * 3 + d - 1
        return remote(q.at[i % 2, at], b_in.at[i, d - 1], b_send.at[n], b_recv.at[n], device(0, 0, d))

    def join(i):
        part_send(i).wait_recv()
        if i >= 2:
            for d in (1, 3, 2):
                b_copy(i - 2, d).wait_send()

        def step(j, carry):
            at = pl.ds(pl.multiple_of(j * 64, 64), 64)
            q[i % 2, at, :] = (part[at, :].astype(F32) + part_in[i % 2, at, :].astype(F32)).astype(BF16)
            return carry

        lax.fori_loop(0, RING, step, 0)
        for d in (2, 1, 3):
            b_copy(i, d).start()

    def a_copy(i):
        return remote(r.at[i], a_in.at[i - 1], a_send.at[i - 1], a_recv.at[i - 1], device(STEPS[i], 0, 0))

    def reduce_b(i):
        for d in (1, 3, 2):
            b_copy(i, d).wait_recv()
        total = q[i % 2, pl.ds(pl.multiple_of(b * 64, 64), 64), :].astype(F32)
        for d in range(3):
            total += b_in[i, d].astype(F32)
        r[i] = total.astype(BF16)
        if i > 0:
            a_copy(i).start()

    def x_copy(d):
        at = pl.ds(pl.multiple_of(plus(x, d) * TOK, TOK), TOK)
        return remote(last.at[at], x_in.at[d - 1], x_send.at[d - 1], x_recv.at[d - 1], device(0, d, 0))

    def out_cols(v):
        return pl.ds(pl.multiple_of(v * cols, 128), cols)

    own(0)
    along_x(0)
    for d in (1, 3, 2):
        send_block(mine, device(d, 0, 0))
    own(1)
    forward(0)
    own(2)
    along_x(1)
    forward(1)
    own(4)
    own(3)
    forward(2)
    along_x(2)
    own(5)
    forward(3)
    own(6)
    forward(4)
    wait_chunk(0)
    select(0)
    along_x(3)
    own(7)
    forward(5)
    own(8)
    forward(6)
    loads[1].wait()
    loads[2].wait()
    gate_up(0)
    own(9)
    forward(7)
    own(10)
    forward(8)
    wait_chunk(1)
    select(1)
    hid_forward(0)
    own(11)
    forward(9)
    own(12)
    forward(10)
    gate_up(1)
    own(13)
    forward(11)
    loads[3].wait()
    finish(0)
    own(14)
    forward(12)
    wait_chunk(2)
    select(2)
    hid_forward(1)
    own(15)
    forward(13)
    join(0)
    gate_up(2)
    forward(14)
    forward(15)
    finish(1)
    reduce_b(0)
    wait_chunk(3)
    select(3)
    join(1)
    hid_forward(2)
    gate_up(3)
    finish(2)
    join(2)
    reduce_b(1)
    hid_forward(3)
    reduce_b(2)
    finish(3)
    join(3)
    reduce_b(3)

    total = r[0].astype(F32)
    for i in (1, 2, 3):
        a_copy(i).wait_recv()
        total += a_in[i - 1].astype(F32)
    last[...] = total.astype(BF16)
    for d in (2, 1, 3):
        x_copy(d).start()
    out_ref[:, out_cols(x)] = last[pl.ds(pl.multiple_of(x * TOK, TOK), TOK), :]
    for d in (1, 3, 2):
        x_copy(d).wait_recv()
        out_ref[:, out_cols(plus(x, RING - d))] = x_in[d - 1]

    for n in range(sent[0]):
        remote(blocks.at[0], blocks.at[0], blk_send.at[n], blk_recv.at[0], sibling).wait_send()
    select_send(3).wait_send()
    part_send(3).wait_send()
    for i in range(4):
        meta_send(i).wait_send()
        for n in range(6):
            hid_copy(i, x, 0, 1, n).wait_send()
        if i >= 2:
            for d in (1, 3, 2):
                b_copy(i, d).wait_send()
        if i > 0:
            a_copy(i).wait_send()
            x_copy(i).wait_send()


def per_device(tokens, expert_ids, gate_weights, w_gate, w_up, w_down):
    rows, width = tokens.shape
    ff = w_gate.shape[2]
    cols = w_down.shape[2]
    dma = pltpu.SemaphoreType.DMA
    vmem = pltpu.VMEM
    return pl.pallas_call(
        kernel,
        out_shape=jax.ShapeDtypeStruct((rows, width), BF16),
        in_specs=[
            pl.BlockSpec(memory_space=pl.ANY),
            pl.BlockSpec(memory_space=pltpu.VMEM),
            pl.BlockSpec(memory_space=pltpu.VMEM),
            pl.BlockSpec(memory_space=pl.ANY),
            pl.BlockSpec(memory_space=pl.ANY),
            pl.BlockSpec(memory_space=pl.ANY),
        ],
        out_specs=pl.BlockSpec(memory_space=pltpu.VMEM),
        scratch_shapes=[
            vmem((width, ff), BF16),
            vmem((width, ff), BF16),
            vmem((RING * ff, cols), BF16),
            vmem((64, TOK, width + META), BF16),
            vmem((256, 256), BF16),
            vmem((2, 256, width), BF16),
            vmem((128, width), BF16),
            vmem((4, 16, TOK, META), BF16),
            vmem((4, RING, 256, ff), BF16),
            vmem((256, 256), BF16),
            vmem((256, 256), BF16),
            vmem((256, cols), BF16),
            vmem((256, cols), BF16),
            vmem((2, 256, cols), BF16),
            vmem((2, 256, cols), BF16),
            vmem((4, 3, 64, cols), BF16),
            vmem((4, 64, cols), BF16),
            vmem((3, 64, cols), BF16),
            vmem((64, cols), BF16),
            vmem((3, TOK, cols), BF16),
            dma((4,)),
            dma((64,)),
            dma((64,)),
            dma((4,)),
            dma((4,)),
            dma((4,)),
            dma((4,)),
            dma((24,)),
            dma((32,)),
            dma((4,)),
            dma((4,)),
            dma((12,)),
            dma((12,)),
            dma((3,)),
            dma((3,)),
            dma((3,)),
            dma((3,)),
        ],
        compiler_params=pltpu.CompilerParams(
            collective_id=0, has_side_effects=True, vmem_limit_bytes=63 * 2**20
        ),
        cost_estimate=pl.CostEstimate(flops=24 * 10**9, bytes_accessed=24 * 10**6, transcendentals=10**6),
    )(tokens, expert_ids.T, gate_weights.T, w_gate, w_up, w_down)


def solution(mesh):
    in_specs = (
        P(("group", "lane"), None),
        P(("group", "lane"), None),
        P(("group", "lane"), None),
        P(("group", "lane"), None, None),
        P(("group", "lane"), None, None),
        P(("group", "lane"), None, None),
    )
    out_specs = P(("group", "lane"), None)
    return jax.shard_map(
        per_device, mesh=mesh, in_specs=in_specs, out_specs=out_specs, check_vma=False
    )
```

```python
import jax
import jax.numpy as jnp
from jax import lax
from jax.experimental import pallas as pl
from jax.experimental.pallas import tpu as pltpu
from jax.sharding import PartitionSpec as P

TOPK = 8
CAP = 8
RING = 4
TOK = 16
META = 128
MESH = pl.DeviceIdType.MESH
BF16 = jnp.bfloat16
F32 = jnp.float32
STEPS = (0, 1, 3, 2)
CHUNKS = (1, 3, 2, 0)


def iota(shape, dim):
    return lax.broadcasted_iota(jnp.int32, shape, dim)


def routing_rows(ids, gates):
    unit = jnp.where(iota((TOPK, TOPK), 0) == iota((TOPK, TOPK), 1), 1.0, 0.0).astype(BF16)

    def turned(values):
        return lax.dot_general(values.astype(BF16), unit, (((0,), (0,)), ((), ())), preferred_element_type=F32)

    ids = turned(ids.astype(F32)).astype(jnp.int32)
    upper = gates.astype(BF16).astype(F32)
    lower = turned(gates - upper)
    upper = turned(upper)
    lane = iota((TOK, META), 1)
    picked = jnp.zeros((TOK, META), F32)
    high = jnp.zeros((TOK, META), F32)
    low = jnp.zeros((TOK, META), F32)
    for k in range(TOPK):
        name = ids[:, k : k + 1]
        picked = jnp.where(lane == name, 1.0, picked)
        high = jnp.where(lane == name + 32, upper[:, k : k + 1], high)
        low = jnp.where(lane == name + 64, lower[:, k : k + 1], low)
    earlier = jnp.where(iota((TOK, TOK), 1) < iota((TOK, TOK), 0), 1.0, 0.0)
    before = jnp.dot(earlier, picked, preferred_element_type=F32)
    slot = jnp.where(picked > 0.5, before, -1.0)
    return jnp.where(lane < 32, slot, jnp.where(lane < 64, high, low)).astype(BF16)


def kernel(
    tok_hbm, ids_ref, gates_ref, wg_hbm, wu_hbm, wd_hbm, out_ref,
    wg, wu, wd, blocks, chooser, rows, sib_out, meta_in, hid, mix_own, mix_sib,
    part, part_out, part_in, q, b_in, r, a_in, last, x_in,
    load_sem, blk_send, blk_recv, sel_send, sel_recv, met_send, met_recv, hid_send, hid_recv,
    prt_send, prt_recv, b_send, b_recv, a_send, a_recv, x_send, x_recv,
):
    width = wg.shape[0]
    ff = wg.shape[1]
    cols = wd.shape[1]
    half = cols // 2
    group, lane_index = lax.axis_index("group"), lax.axis_index("lane")
    z, c = group // 2, lax.rem(group, 2)
    y, x = lane_index // RING, lax.rem(lane_index, RING)
    a = (1 - c) * y + c * z
    b = (1 - c) * z + c * y

    def plus(v, d):
        return lax.rem(v + d, RING)

    def device(da, dx, db):
        a2, b2 = plus(a, da), plus(b, db)
        return (((1 - c) * b2 + c * a2) * 2 + c, ((1 - c) * a2 + c * b2) * RING + plus(x, dx))

    def place(da, dx, db):
        return plus(a, da) * (RING * RING) + plus(x, dx) * RING + plus(b, db)

    sibling = (z * 2 + 1 - c, lane_index)
    own_expert = group * RING + y
    sib_expert = (z * 2 + 1 - c) * RING + y

    def remote(src, dst, send, recv, target):
        return pltpu.make_async_remote_copy(
            src_ref=src, dst_ref=dst, send_sem=send, recv_sem=recv, device_id=target, device_id_type=MESH
        )

    mine = place(0, 0, 0)
    loads = [
        pltpu.make_async_copy(tok_hbm, blocks.at[mine, :, pl.ds(0, width)], load_sem.at[0]),
        pltpu.make_async_copy(wg_hbm.at[0], wg, load_sem.at[1]),
        pltpu.make_async_copy(wu_hbm.at[0], wu, load_sem.at[2]),
        pltpu.make_async_copy(wd_hbm.at[0], wd, load_sem.at[3]),
    ]
    for load in loads:
        load.start()

    peers = [sibling]
    for d in (1, 3, 2):
        peers += [device(d, 0, 0), device(0, d, 0), device(0, 0, d)]
    barrier = pltpu.get_barrier_semaphore()
    for peer in peers:
        pl.semaphore_signal(barrier, inc=1, device_id=peer, device_id_type=MESH)

    blocks[mine, :, pl.ds(width, META)] = routing_rows(ids_ref[...], gates_ref[...])
    loads[0].wait()
    pl.semaphore_wait(barrier, len(peers))

    sent = [0]
    order = [(da, dx) for da in CHUNKS for dx in STEPS]

    def send_block(s, target):
        remote(blocks.at[s], blocks.at[s], blk_send.at[sent[0]], blk_recv.at[s], target).start()
        sent[0] += 1

    def wait_block(s):
        remote(blocks.at[s], blocks.at[s], blk_send.at[0], blk_recv.at[s], sibling).wait_recv()

    def along_x(i):
        s = place(CHUNKS[i], 0, 0)
        if CHUNKS[i] != 0:
            wait_block(s)
        send_block(s, device(0, 1, 0))
        send_block(s, device(0, 3, 0))

    def spot(k, db):
        da, dx = order[k]
        if k < 3 * RING:
            return place(da, dx, db)
        return plus(a, da) * (RING * RING) + (k % RING) * RING + plus(b, db)

    def across(k):
        da, dx = order[k]
        s = place(da, dx, 0)
        if dx != 0:
            wait_block(s)
        if dx == (3, 1)[k // RING % 2]:
            send_block(s, device(0, RING - dx, 0))

    def own(k):
        if k < 3 * RING:
            across(k)
        s = spot(k, 0)
        send_block(s, device(0, 0, 1))
        send_block(s, device(0, 0, 3))

    def forward(k):
        came, goes = (3, 1) if k % 2 == 0 else (1, 3)
        s = spot(k, came)
        wait_block(s)
        send_block(s, device(0, 0, goes))

    blocks_in = (16, 16, 16, 8, 8)
    chunk_of = (0, 1, 2, 3, 3)
    first = (0, 0, 0, 0, 2)

    def wait_chunk(i):
        begin = chunk_of[i] * RING + first[i]
        for k in range(begin, begin + blocks_in[i] // RING):
            for db in (1, 3, 2):
                if db != (3, 1)[k % 2]:
                    wait_block(spot(k, db))

    def chunk(i):
        return pl.ds(plus(a, CHUNKS[chunk_of[i]]) * (RING * RING) + first[i] * RING, blocks_in[i])

    def over_x(i):
        return pl.ds(first[i], blocks_in[i] // RING)

    def select_send(i):
        n = blocks_in[i] * CAP
        return remote(sib_out.at[pl.ds(0, n)], rows.at[i % 2, pl.ds(n, n)], sel_send.at[i], sel_recv.at[i], sibling)

    def meta_send(i):
        return remote(
            blocks.at[chunk(i), :, pl.ds(width, META)], meta_in.at[i, pl.ds(0, blocks_in[i])], met_send.at[i], met_recv.at[i], sibling
        )

    def select(i):
        n, m = blocks_in[i] * CAP, blocks_in[i] * TOK
        meta = blocks[chunk(i), :, pl.ds(width, META)].reshape(m, META)
        row, lane = iota((16, META), 0), iota((16, META), 1)
        want = jnp.where(row == 0, own_expert, sib_expert)
        pick = jnp.where(lane == want, 1.0, 0.0).astype(BF16)
        slots = lax.dot_general(pick, meta, (((1,), (1,)), ((), ())), preferred_element_type=F32)
        row, col = iota((m, m), 0), iota((m, m), 1)
        slot = jnp.where(row < n, slots[0:1, :], slots[1:2, :])
        same = ((row & (n - 1)) >> 3) == (col >> 4)
        taken = slot == (row & 7).astype(F32)
        chooser[pl.ds(0, m), pl.ds(0, m)] = jnp.where(same & taken, 1.0, 0.0).astype(BF16)
        if i > 0:
            select_send(i - 1).wait_send()

        def step(j, carry):
            at = pl.ds(pl.multiple_of(j * 1024, 1024), 1024)
            tokens = blocks[chunk(i), :, at].reshape(m, 1024)
            got = jnp.dot(chooser[pl.ds(0, m), pl.ds(0, m)], tokens, preferred_element_type=F32).astype(BF16)
            rows[i % 2, pl.ds(0, n), at] = got[:n]
            sib_out[pl.ds(0, n), at] = got[n:]
            return carry

        lax.fori_loop(0, width // 1024, step, 0)
        select_send(i).start()
        meta_send(i).start()

    def hid_rows(i):
        return pl.ds(first[i] * 64, blocks_in[i] * TOK)

    def hid_copy(i, owner, h, target, n):
        at = hid.at[chunk_of[i], owner, h, hid_rows(i)]
        return remote(at, at, hid_send.at[i * 6 + n], hid_recv.at[(i * RING + owner) * 2 + h], device(0, target, 0))

    def gate_up(i, h):
        if h == 0:
            select_send(i).wait_recv()
        at = pl.ds(h * 256, 256)
        chosen = rows.at[i % 2, pl.ds(0, blocks_in[i] * TOK)]
        gate = jnp.dot(chosen[...], wg[:, at], preferred_element_type=F32)
        up = jnp.dot(chosen[...], wu[:, at], preferred_element_type=F32)
        hid[chunk_of[i], x, h, hid_rows(i)] = (gate / (1.0 + jnp.exp(-gate)) * up).astype(BF16)
        hid_copy(i, x, h, (1, 3)[h], h).start()
        hid_copy(i, x, h, (3, 1)[h], 2 + h).start()

    def hid_forward(i, h):
        came, goes = ((3, 1), (1, 3))[h]
        hid_copy(i, plus(x, came), h, goes, 4 + h).wait_recv()
        hid_copy(i, plus(x, came), h, goes, 4 + h).start()

    def mixer(meta, n, m):
        meta = meta.reshape(m, META).astype(F32)
        lane = iota((m, META), 1)

        def column(at):
            return jnp.sum(jnp.where(lane == at, meta, 0.0), axis=1, keepdims=True)

        slot, high, low = column(own_expert), column(own_expert + 32), column(own_expert + 64)
        row, col = iota((m, m), 0), iota((m, m), 1)
        same = (row >> 4) == ((col & (n - 1)) >> 3)
        taken = slot == (col & 7).astype(F32)
        return jnp.where(same & taken, jnp.where(col < n, high, low), 0.0).astype(BF16)

    def part_send(i, j):
        n, count = i * 2 + j, pl.ds(0, blocks_in[i] // RING)
        return remote(part_out.at[j, count], part_in.at[i % 2, j, count], prt_send.at[n], prt_recv.at[n], sibling)

    def weigh(i):
        n, m = blocks_in[i] * CAP, blocks_in[i] * TOK
        meta_send(i).wait_recv()
        at = pl.ds(0, m)
        mix_own[at, at] = mixer(blocks[chunk(i), :, pl.ds(width, META)], n, m)
        mix_sib[at, at] = mixer(meta_in[i, pl.ds(0, blocks_in[i])], n, m)

    def finish(i, j):
        if j == 0:
            hid_copy(i, plus(x, 3), 1, 1, 0).wait_recv()
            hid_copy(i, plus(x, 1), 0, 1, 0).wait_recv()
            hid_copy(i, plus(x, 2), 0, 1, 0).wait_recv()
            hid_copy(i, plus(x, 2), 1, 1, 0).wait_recv()
        n, m = blocks_in[i] * CAP, blocks_in[i] * TOK
        at, count = pl.ds(0, m), pl.ds(0, blocks_in[i] // RING)
        shape = (blocks_in[i] // RING, RING, TOK, half)
        hidden = jnp.concatenate([hid[chunk_of[i], s, h, hid_rows(i)] for s in range(RING) for h in range(2)], axis=1)
        total = jnp.dot(hidden, wd[:, pl.ds(j * half, half)], preferred_element_type=F32).astype(BF16)
        for_own = jnp.concatenate([total[:n], total[:n]], axis=0)
        for_sib = jnp.concatenate([total[n:], total[n:]], axis=0)
        if i > 0:
            part_send(i - 1, j).wait_send()
        mixed = jnp.dot(mix_sib[at, at], for_sib, preferred_element_type=F32).astype(BF16)
        part_out[j, count] = mixed.reshape(shape)
        part_send(i, j).start()
        mixed = jnp.dot(mix_own[at, at], for_own, preferred_element_type=F32).astype(BF16)
        part[j, count] = mixed.reshape(shape)

    def b_copy(i, d, j):
        n = (i * 3 + d - 1) * 2 + j
        return remote(
            q.at[i % 2, j, pl.ds(0, blocks_in[i] // RING), plus(b, d)], b_in.at[chunk_of[i], d - 1, j, over_x(i)],
            b_send.at[n], b_recv.at[n], device(0, 0, d),
        )

    def join(i, j):
        part_send(i, j).wait_recv()
        if i >= 2:
            for d in (1, 3, 2):
                b_copy(i - 2, d, j).wait_send()

        def step(n, carry):
            q[i % 2, j, n] = (part[j, n].astype(F32) + part_in[i % 2, j, n].astype(F32)).astype(BF16)
            return carry

        lax.fori_loop(0, blocks_in[i] // RING, step, 0)
        for d in (2, 1, 3):
            b_copy(i, d, j).start()

    def a_copy(i, j):
        n = i * 2 + j
        return remote(r.at[i, j], a_in.at[i, j], a_send.at[n], a_recv.at[n], device(CHUNKS[i], 0, 0))

    def reduce(i, j):
        for d in (1, 3, 2):
            b_copy(i, d, j).wait_recv()
        total = q[i % 2, j, pl.ds(0, blocks_in[i] // RING), b].astype(F32)
        for d in range(3):
            total += b_in[chunk_of[i], d, j, over_x(i)].astype(F32)
        if i < 3:
            r[i, j] = total.astype(BF16)
            a_copy(i, j).start()
            return
        for n in range(3):
            if i == 3:
                a_copy(n, j).wait_recv()
            total += a_in[n, j, over_x(i)].astype(F32)
        last[j, over_x(i)] = total.astype(BF16)
        if i == 4:
            for d in (2, 1, 3):
                x_copy(d, j).start()

    def x_copy(d, j):
        n = (d - 1) * 2 + j
        return remote(last.at[j, plus(x, d)], x_in.at[d - 1, j], x_send.at[n], x_recv.at[n], device(0, d, 0))

    def out_cols(v, j):
        return pl.ds(pl.multiple_of(v * cols + j * half, 128), half)

    for d in (3, 1, 2):
        send_block(mine, device(d, 0, 0))
    along_x(0)
    own(0)
    own(1)
    forward(0)
    own(2)
    along_x(1)
    forward(1)
    own(4)
    own(3)
    forward(2)
    along_x(2)
    own(5)
    forward(3)
    own(6)
    forward(4)
    along_x(3)
    own(7)
    forward(5)
    own(8)
    forward(6)
    wait_chunk(0)
    select(0)
    own(9)
    forward(7)
    own(10)
    forward(8)
    loads[1].wait()
    loads[2].wait()
    gate_up(0, 0)
    across(13)
    across(14)
    own(11)
    forward(9)
    gate_up(0, 1)
    across(15)
    own(12)
    forward(10)
    wait_chunk(1)
    select(1)
    hid_forward(0, 0)
    own(13)
    forward(11)
    hid_forward(0, 1)
    own(14)
    forward(12)
    gate_up(1, 0)
    own(15)
    forward(13)
    gate_up(1, 1)
    forward(14)
    wait_chunk(2)
    select(2)
    forward(15)
    hid_forward(1, 0)
    weigh(0)
    loads[3].wait()
    finish(0, 0)
    finish(0, 1)
    hid_forward(1, 1)
    gate_up(2, 0)
    gate_up(2, 1)
    wait_chunk(3)
    select(3)
    join(0, 0)
    join(0, 1)
    weigh(1)
    finish(1, 0)
    finish(1, 1)
    hid_forward(2, 0)
    hid_forward(2, 1)
    gate_up(3, 0)
    gate_up(3, 1)
    wait_chunk(4)
    select(4)
    join(1, 0)
    join(1, 1)
    reduce(0, 0)
    reduce(0, 1)
    weigh(2)
    finish(2, 0)
    finish(2, 1)
    gate_up(4, 0)
    gate_up(4, 1)
    hid_forward(3, 0)
    hid_forward(3, 1)
    join(2, 0)
    join(2, 1)
    reduce(1, 0)
    reduce(1, 1)
    weigh(3)
    finish(3, 0)
    finish(3, 1)
    hid_forward(4, 0)
    hid_forward(4, 1)
    join(3, 0)
    join(3, 1)
    reduce(2, 0)
    reduce(2, 1)
    weigh(4)
    finish(4, 0)
    finish(4, 1)
    join(4, 0)
    join(4, 1)
    reduce(3, 0)
    reduce(3, 1)
    reduce(4, 0)
    reduce(4, 1)

    for j in range(2):
        out_ref[:, out_cols(x, j)] = last[j, x]
        for d in (1, 3, 2):
            x_copy(d, j).wait_recv()
            out_ref[:, out_cols(plus(x, RING - d), j)] = x_in[d - 1, j]

    for n in range(sent[0]):
        remote(blocks.at[0], blocks.at[0], blk_send.at[n], blk_recv.at[0], sibling).wait_send()
    select_send(4).wait_send()
    for i in range(5):
        meta_send(i).wait_send()
        for n in range(6):
            hid_copy(i, x, 0, 1, n).wait_send()
    for j in range(2):
        part_send(4, j).wait_send()
        for d in (1, 3, 2):
            b_copy(4, d, j).wait_send()
            b_copy(3, d, j).wait_send()
            a_copy(d - 1, j).wait_send()
            x_copy(d, j).wait_send()


def per_device(tokens, expert_ids, gate_weights, w_gate, w_up, w_down):
    rows, width = tokens.shape
    ff = w_gate.shape[2]
    cols = w_down.shape[2]
    half = cols // 2
    dma = pltpu.SemaphoreType.DMA
    vmem = pltpu.VMEM
    return pl.pallas_call(
        kernel,
        out_shape=jax.ShapeDtypeStruct((rows, width), BF16),
        in_specs=[
            pl.BlockSpec(memory_space=pl.ANY),
            pl.BlockSpec(memory_space=pltpu.VMEM),
            pl.BlockSpec(memory_space=pltpu.VMEM),
            pl.BlockSpec(memory_space=pl.ANY),
            pl.BlockSpec(memory_space=pl.ANY),
            pl.BlockSpec(memory_space=pl.ANY),
        ],
        out_specs=pl.BlockSpec(memory_space=pltpu.VMEM),
        scratch_shapes=[
            vmem((width, ff), BF16),
            vmem((width, ff), BF16),
            vmem((RING * ff, cols), BF16),
            vmem((64, TOK, width + META), BF16),
            vmem((256, 256), BF16),
            vmem((2, 256, width), BF16),
            vmem((128, width), BF16),
            vmem((5, 16, TOK, META), BF16),
            vmem((4, RING, 2, 256, 256), BF16),
            vmem((256, 256), BF16),
            vmem((256, 256), BF16),
            vmem((2, RING, RING, TOK, half), BF16),
            vmem((2, RING, RING, TOK, half), BF16),
            vmem((2, 2, RING, RING, TOK, half), BF16),
            vmem((2, 2, RING, RING, TOK, half), BF16),
            vmem((4, 3, 2, RING, TOK, half), BF16),
            vmem((3, 2, RING, TOK, half), BF16),
            vmem((3, 2, RING, TOK, half), BF16),
            vmem((2, RING, TOK, half), BF16),
            vmem((3, 2, TOK, half), BF16),
            dma((4,)),
            dma((64,)),
            dma((64,)),
            dma((5,)),
            dma((5,)),
            dma((5,)),
            dma((5,)),
            dma((30,)),
            dma((40,)),
            dma((10,)),
            dma((10,)),
            dma((30,)),
            dma((30,)),
            dma((6,)),
            dma((6,)),
            dma((6,)),
            dma((6,)),
        ],
        compiler_params=pltpu.CompilerParams(
            collective_id=0, has_side_effects=True, vmem_limit_bytes=63 * 2**20
        ),
        cost_estimate=pl.CostEstimate(flops=24 * 10**9, bytes_accessed=24 * 10**6, transcendentals=10**6),
    )(tokens, expert_ids.T, gate_weights.T, w_gate, w_up, w_down)


def solution(mesh):
    in_specs = (
        P(("group", "lane"), None),
        P(("group", "lane"), None),
        P(("group", "lane"), None),
        P(("group", "lane"), None, None),
        P(("group", "lane"), None, None),
        P(("group", "lane"), None, None),
    )
    out_specs = P(("group", "lane"), None)
    return jax.shard_map(
        per_device, mesh=mesh, in_specs=in_specs, out_specs=out_specs, check_vma=False
    )
```

```python
import jax
import jax.numpy as jnp
from jax import lax
from jax.experimental import pallas as pl
from jax.experimental.pallas import tpu as pltpu
from jax.sharding import PartitionSpec as P

TOPK = 8
CAP = 8
RING = 4
TOK = 16
META = 128
MESH = pl.DeviceIdType.MESH
BF16 = jnp.bfloat16
F32 = jnp.float32
STEPS = (0, 1, 3, 2)
CHUNKS = (1, 3, 2, 0)


def iota(shape, dim):
    return lax.broadcasted_iota(jnp.int32, shape, dim)


def routing_rows(ids, gates):
    unit = jnp.where(iota((TOPK, TOPK), 0) == iota((TOPK, TOPK), 1), 1.0, 0.0).astype(BF16)

    def turned(values):
        return lax.dot_general(values.astype(BF16), unit, (((0,), (0,)), ((), ())), preferred_element_type=F32)

    ids = turned(ids.astype(F32)).astype(jnp.int32)
    upper = gates.astype(BF16).astype(F32)
    lower = turned(gates - upper)
    upper = turned(upper)
    lane = iota((TOK, META), 1)
    picked = jnp.zeros((TOK, META), F32)
    high = jnp.zeros((TOK, META), F32)
    low = jnp.zeros((TOK, META), F32)
    for k in range(TOPK):
        name = ids[:, k : k + 1]
        picked = jnp.where(lane == name, 1.0, picked)
        high = jnp.where(lane == name + 32, upper[:, k : k + 1], high)
        low = jnp.where(lane == name + 64, lower[:, k : k + 1], low)
    earlier = jnp.where(iota((TOK, TOK), 1) < iota((TOK, TOK), 0), 1.0, 0.0)
    before = jnp.dot(earlier, picked, preferred_element_type=F32)
    slot = jnp.where(picked > 0.5, before, -1.0)
    return jnp.where(lane < 32, slot, jnp.where(lane < 64, high, low)).astype(BF16)


def kernel(
    tok_hbm, ids_ref, gates_ref, wg_hbm, wu_hbm, wd_hbm, out_ref,
    wg, wu, wd, blocks, chooser, rows, sib_out, meta_in, hid, mix_own, mix_sib,
    part, part_out, part_in, q, b_in, r, a_in, last, x_in,
    load_sem, blk_send, blk_recv, sel_send, sel_recv, met_send, met_recv, hid_send, hid_recv,
    prt_send, prt_recv, b_send, b_recv, a_send, a_recv, x_send, x_recv,
):
    width = wg.shape[0]
    ff = wg.shape[1]
    cols = wd.shape[1]
    half = cols // 2
    group, lane_index = lax.axis_index("group"), lax.axis_index("lane")
    z, c = group // 2, lax.rem(group, 2)
    y, x = lane_index // RING, lax.rem(lane_index, RING)
    a = (1 - c) * y + c * z
    b = (1 - c) * z + c * y

    def plus(v, d):
        return lax.rem(v + d, RING)

    def device(da, dx, db):
        a2, b2 = plus(a, da), plus(b, db)
        return (((1 - c) * b2 + c * a2) * 2 + c, ((1 - c) * a2 + c * b2) * RING + plus(x, dx))

    def place(da, dx, db):
        return plus(a, da) * (RING * RING) + plus(x, dx) * RING + plus(b, db)

    sibling = (z * 2 + 1 - c, lane_index)
    own_expert = group * RING + y
    sib_expert = (z * 2 + 1 - c) * RING + y

    def remote(src, dst, send, recv, target):
        return pltpu.make_async_remote_copy(
            src_ref=src, dst_ref=dst, send_sem=send, recv_sem=recv, device_id=target, device_id_type=MESH
        )

    mine = place(0, 0, 0)
    loads = [
        pltpu.make_async_copy(tok_hbm, blocks.at[mine, :, pl.ds(0, width)], load_sem.at[0]),
        pltpu.make_async_copy(wg_hbm.at[0], wg, load_sem.at[1]),
        pltpu.make_async_copy(wu_hbm.at[0], wu, load_sem.at[2]),
        pltpu.make_async_copy(wd_hbm.at[0], wd, load_sem.at[3]),
    ]
    for load in loads:
        load.start()

    peers = [sibling]
    for d in (1, 3, 2):
        peers += [device(d, 0, 0), device(0, d, 0), device(0, 0, d)]
    barrier = pltpu.get_barrier_semaphore()
    for peer in peers:
        pl.semaphore_signal(barrier, inc=1, device_id=peer, device_id_type=MESH)

    blocks[mine, :, pl.ds(width, META)] = routing_rows(ids_ref[...], gates_ref[...])
    loads[0].wait()
    pl.semaphore_wait(barrier, len(peers))

    sent = [0]
    order = [(da, dx) for da in CHUNKS for dx in STEPS]

    def send_block(s, target):
        remote(blocks.at[s], blocks.at[s], blk_send.at[sent[0]], blk_recv.at[s], target).start()
        sent[0] += 1

    def wait_block(s):
        remote(blocks.at[s], blocks.at[s], blk_send.at[0], blk_recv.at[s], sibling).wait_recv()

    def along_x(i):
        s = place(CHUNKS[i], 0, 0)
        if CHUNKS[i] != 0:
            wait_block(s)
        send_block(s, device(0, 1, 0))
        send_block(s, device(0, 3, 0))

    def spot(k, db):
        da, dx = order[k]
        if k < 3 * RING:
            return place(da, dx, db)
        return plus(a, da) * (RING * RING) + (k % RING) * RING + plus(b, db)

    def across(k):
        da, dx = order[k]
        s = place(da, dx, 0)
        if dx != 0:
            wait_block(s)
        if dx == (3, 1)[k // RING % 2]:
            send_block(s, device(0, RING - dx, 0))

    def own(k):
        if k < 3 * RING:
            across(k)
        s = spot(k, 0)
        send_block(s, device(0, 0, 1))
        send_block(s, device(0, 0, 3))

    def forward(k):
        came, goes = (3, 1) if k % 2 == 0 else (1, 3)
        s = spot(k, came)
        wait_block(s)
        send_block(s, device(0, 0, goes))

    blocks_in = (16, 16, 16, 8, 8)
    chunk_of = (0, 1, 2, 3, 3)
    first = (0, 0, 0, 0, 2)

    def wait_chunk(i):
        begin = chunk_of[i] * RING + first[i]
        for k in range(begin, begin + blocks_in[i] // RING):
            for db in (1, 3, 2):
                if db != (3, 1)[k % 2]:
                    wait_block(spot(k, db))

    def chunk(i):
        return pl.ds(plus(a, CHUNKS[chunk_of[i]]) * (RING * RING) + first[i] * RING, blocks_in[i])

    def over_x(i):
        return pl.ds(first[i], blocks_in[i] // RING)

    def select_send(i):
        n = blocks_in[i] * CAP
        return remote(sib_out.at[pl.ds(0, n)], rows.at[i % 2, pl.ds(n, n)], sel_send.at[i], sel_recv.at[i], sibling)

    def meta_send(i):
        return remote(
            blocks.at[chunk(i), :, pl.ds(width, META)], meta_in.at[i, pl.ds(0, blocks_in[i])], met_send.at[i], met_recv.at[i], sibling
        )

    def select(i):
        n, m = blocks_in[i] * CAP, blocks_in[i] * TOK
        meta = blocks[chunk(i), :, pl.ds(width, META)].reshape(m, META)
        row, lane = iota((16, META), 0), iota((16, META), 1)
        want = jnp.where(row == 0, own_expert, sib_expert)
        pick = jnp.where(lane == want, 1.0, 0.0).astype(BF16)
        slots = lax.dot_general(pick, meta, (((1,), (1,)), ((), ())), preferred_element_type=F32)
        row, col = iota((m, m), 0), iota((m, m), 1)
        slot = jnp.where(row < n, slots[0:1, :], slots[1:2, :])
        same = ((row & (n - 1)) >> 3) == (col >> 4)
        taken = slot == (row & 7).astype(F32)
        chooser[pl.ds(0, m), pl.ds(0, m)] = jnp.where(same & taken, 1.0, 0.0).astype(BF16)
        if i > 0:
            select_send(i - 1).wait_send()

        def step(j, carry):
            at = pl.ds(pl.multiple_of(j * 1024, 1024), 1024)
            tokens = blocks[chunk(i), :, at].reshape(m, 1024)
            got = jnp.dot(chooser[pl.ds(0, m), pl.ds(0, m)], tokens, preferred_element_type=F32).astype(BF16)
            rows[i % 2, pl.ds(0, n), at] = got[:n]
            sib_out[pl.ds(0, n), at] = got[n:]
            return carry

        lax.fori_loop(0, width // 1024, step, 0)
        select_send(i).start()
        meta_send(i).start()

    def hid_rows(i):
        return pl.ds(first[i] * 64, blocks_in[i] * TOK)

    def hid_copy(i, owner, h, target, n):
        at = hid.at[chunk_of[i], owner, h, hid_rows(i)]
        return remote(at, at, hid_send.at[i * 6 + n], hid_recv.at[(i * RING + owner) * 2 + h], device(0, target, 0))

    def gate_up(i, h):
        if h == 0:
            select_send(i).wait_recv()
        at = pl.ds(h * 256, 256)
        chosen = rows.at[i % 2, pl.ds(0, blocks_in[i] * TOK)]
        gate = jnp.dot(chosen[...], wg[:, at], preferred_element_type=F32)
        up = jnp.dot(chosen[...], wu[:, at], preferred_element_type=F32)
        hid[chunk_of[i], x, h, hid_rows(i)] = (gate / (1.0 + jnp.exp(-gate)) * up).astype(BF16)
        hid_copy(i, x, h, (1, 3)[h], h).start()
        hid_copy(i, x, h, (3, 1)[h], 2 + h).start()

    def hid_forward(i, h):
        came, goes = ((3, 1), (1, 3))[h]
        hid_copy(i, plus(x, came), h, goes, 4 + h).wait_recv()
        hid_copy(i, plus(x, came), h, goes, 4 + h).start()

    def mixer(meta, n, m):
        meta = meta.reshape(m, META).astype(F32)
        lane = iota((m, META), 1)

        def column(at):
            return jnp.sum(jnp.where(lane == at, meta, 0.0), axis=1, keepdims=True)

        slot, high, low = column(own_expert), column(own_expert + 32), column(own_expert + 64)
        row, col = iota((m, m), 0), iota((m, m), 1)
        same = (row >> 4) == ((col & (n - 1)) >> 3)
        taken = slot == (col & 7).astype(F32)
        return jnp.where(same & taken, jnp.where(col < n, high, low), 0.0).astype(BF16)

    def part_send(i, j):
        n, count = i * 2 + j, pl.ds(0, blocks_in[i] // RING)
        return remote(part_out.at[j, count], part_in.at[i % 2, j, count], prt_send.at[n], prt_recv.at[n], sibling)

    def weigh(i):
        n, m = blocks_in[i] * CAP, blocks_in[i] * TOK
        meta_send(i).wait_recv()
        at = pl.ds(0, m)
        mix_own[at, at] = mixer(blocks[chunk(i), :, pl.ds(width, META)], n, m)
        mix_sib[at, at] = mixer(meta_in[i, pl.ds(0, blocks_in[i])], n, m)

    def finish(i, j):
        if j == 0:
            hid_copy(i, plus(x, 3), 1, 1, 0).wait_recv()
            hid_copy(i, plus(x, 1), 0, 1, 0).wait_recv()
            hid_copy(i, plus(x, 2), 0, 1, 0).wait_recv()
            hid_copy(i, plus(x, 2), 1, 1, 0).wait_recv()
        n, m = blocks_in[i] * CAP, blocks_in[i] * TOK
        at, count = pl.ds(0, m), pl.ds(0, blocks_in[i] // RING)
        shape = (blocks_in[i] // RING, RING, TOK, half)
        hidden = jnp.concatenate([hid[chunk_of[i], s, h, hid_rows(i)] for s in range(RING) for h in range(2)], axis=1)
        total = jnp.dot(hidden, wd[:, pl.ds(j * half, half)], preferred_element_type=F32).astype(BF16)
        for_own = jnp.concatenate([total[:n], total[:n]], axis=0)
        for_sib = jnp.concatenate([total[n:], total[n:]], axis=0)
        if i > 0:
            part_send(i - 1, j).wait_send()
        mixed = jnp.dot(mix_sib[at, at], for_sib, preferred_element_type=F32).astype(BF16)
        part_out[j, count] = mixed.reshape(shape)
        part_send(i, j).start()
        mixed = jnp.dot(mix_own[at, at], for_own, preferred_element_type=F32).astype(BF16)
        part[j, count] = mixed.reshape(shape)

    def b_copy(i, d, j):
        n = (i * 3 + d - 1) * 2 + j
        return remote(
            q.at[i % 2, j, pl.ds(0, blocks_in[i] // RING), plus(b, d)], b_in.at[chunk_of[i], d - 1, j, over_x(i)],
            b_send.at[n], b_recv.at[n], device(0, 0, d),
        )

    def join(i, j):
        part_send(i, j).wait_recv()
        if i >= 2:
            for d in (1, 3, 2):
                b_copy(i - 2, d, j).wait_send()

        def step(n, carry):
            q[i % 2, j, n] = (part[j, n].astype(F32) + part_in[i % 2, j, n].astype(F32)).astype(BF16)
            return carry

        lax.fori_loop(0, blocks_in[i] // RING, step, 0)
        for d in (2, 1, 3):
            b_copy(i, d, j).start()

    def a_copy(i, j):
        n = i * 2 + j
        return remote(r.at[i, j], a_in.at[i, j], a_send.at[n], a_recv.at[n], device(CHUNKS[i], 0, 0))

    def reduce(i, j):
        for d in (1, 3, 2):
            b_copy(i, d, j).wait_recv()
        total = q[i % 2, j, pl.ds(0, blocks_in[i] // RING), b].astype(F32)
        for d in range(3):
            total += b_in[chunk_of[i], d, j, over_x(i)].astype(F32)
        if i < 3:
            r[i, j] = total.astype(BF16)
            a_copy(i, j).start()
            return
        for n in range(3):
            if i == 3:
                a_copy(n, j).wait_recv()
            total += a_in[n, j, over_x(i)].astype(F32)
        last[j, over_x(i)] = total.astype(BF16)
        if i == 4:
            for d in (2, 1, 3):
                x_copy(d, j).start()

    def x_copy(d, j):
        n = (d - 1) * 2 + j
        return remote(last.at[j, plus(x, d)], x_in.at[d - 1, j], x_send.at[n], x_recv.at[n], device(0, d, 0))

    def out_cols(v, j):
        return pl.ds(pl.multiple_of(v * cols + j * half, 128), half)

    for d in (3, 1, 2):
        send_block(mine, device(d, 0, 0))
    along_x(0)
    own(0)
    own(1)
    forward(0)
    own(2)
    along_x(1)
    forward(1)
    own(4)
    own(3)
    forward(2)
    along_x(2)
    own(5)
    forward(3)
    own(6)
    forward(4)
    along_x(3)
    own(7)
    forward(5)
    own(8)
    forward(6)
    wait_chunk(0)
    select(0)
    own(9)
    forward(7)
    own(10)
    forward(8)
    loads[1].wait()
    loads[2].wait()
    gate_up(0, 0)
    across(13)
    across(14)
    own(11)
    forward(9)
    gate_up(0, 1)
    across(15)
    own(12)
    forward(10)
    wait_chunk(1)
    select(1)
    hid_forward(0, 0)
    own(13)
    forward(11)
    hid_forward(0, 1)
    own(14)
    forward(12)
    gate_up(1, 0)
    own(15)
    gate_up(1, 1)
    forward(13)
    wait_chunk(2)
    select(2)
    hid_forward(1, 0)
    weigh(0)
    forward(14)
    loads[3].wait()
    finish(0, 0)
    forward(15)
    finish(0, 1)
    hid_forward(1, 1)
    gate_up(2, 0)
    gate_up(2, 1)
    wait_chunk(3)
    select(3)
    join(0, 0)
    join(0, 1)
    weigh(1)
    finish(1, 0)
    finish(1, 1)
    hid_forward(2, 0)
    hid_forward(2, 1)
    gate_up(3, 0)
    gate_up(3, 1)
    wait_chunk(4)
    select(4)
    join(1, 0)
    join(1, 1)
    reduce(0, 0)
    reduce(0, 1)
    weigh(2)
    finish(2, 0)
    finish(2, 1)
    gate_up(4, 0)
    gate_up(4, 1)
    hid_forward(3, 0)
    hid_forward(3, 1)
    join(2, 0)
    join(2, 1)
    reduce(1, 0)
    reduce(1, 1)
    weigh(3)
    finish(3, 0)
    finish(3, 1)
    hid_forward(4, 0)
    hid_forward(4, 1)
    join(3, 0)
    join(3, 1)
    reduce(2, 0)
    reduce(2, 1)
    weigh(4)
    finish(4, 0)
    finish(4, 1)
    join(4, 0)
    join(4, 1)
    reduce(3, 0)
    reduce(3, 1)
    reduce(4, 0)
    reduce(4, 1)

    for j in range(2):
        out_ref[:, out_cols(x, j)] = last[j, x]
        for d in (1, 3, 2):
            x_copy(d, j).wait_recv()
            out_ref[:, out_cols(plus(x, RING - d), j)] = x_in[d - 1, j]

    for n in range(sent[0]):
        remote(blocks.at[0], blocks.at[0], blk_send.at[n], blk_recv.at[0], sibling).wait_send()
    select_send(4).wait_send()
    for i in range(5):
        meta_send(i).wait_send()
        for n in range(6):
            hid_copy(i, x, 0, 1, n).wait_send()
    for j in range(2):
        part_send(4, j).wait_send()
        for d in (1, 3, 2):
            b_copy(4, d, j).wait_send()
            b_copy(3, d, j).wait_send()
            a_copy(d - 1, j).wait_send()
            x_copy(d, j).wait_send()


def per_device(tokens, expert_ids, gate_weights, w_gate, w_up, w_down):
    rows, width = tokens.shape
    ff = w_gate.shape[2]
    cols = w_down.shape[2]
    half = cols // 2
    dma = pltpu.SemaphoreType.DMA
    vmem = pltpu.VMEM
    return pl.pallas_call(
        kernel,
        out_shape=jax.ShapeDtypeStruct((rows, width), BF16),
        in_specs=[
            pl.BlockSpec(memory_space=pl.ANY),
            pl.BlockSpec(memory_space=pltpu.VMEM),
            pl.BlockSpec(memory_space=pltpu.VMEM),
            pl.BlockSpec(memory_space=pl.ANY),
            pl.BlockSpec(memory_space=pl.ANY),
            pl.BlockSpec(memory_space=pl.ANY),
        ],
        out_specs=pl.BlockSpec(memory_space=pltpu.VMEM),
        scratch_shapes=[
            vmem((width, ff), BF16),
            vmem((width, ff), BF16),
            vmem((RING * ff, cols), BF16),
            vmem((64, TOK, width + META), BF16),
            vmem((256, 256), BF16),
            vmem((2, 256, width), BF16),
            vmem((128, width), BF16),
            vmem((5, 16, TOK, META), BF16),
            vmem((4, RING, 2, 256, 256), BF16),
            vmem((256, 256), BF16),
            vmem((256, 256), BF16),
            vmem((2, RING, RING, TOK, half), BF16),
            vmem((2, RING, RING, TOK, half), BF16),
            vmem((2, 2, RING, RING, TOK, half), BF16),
            vmem((2, 2, RING, RING, TOK, half), BF16),
            vmem((4, 3, 2, RING, TOK, half), BF16),
            vmem((3, 2, RING, TOK, half), BF16),
            vmem((3, 2, RING, TOK, half), BF16),
            vmem((2, RING, TOK, half), BF16),
            vmem((3, 2, TOK, half), BF16),
            dma((4,)),
            dma((64,)),
            dma((64,)),
            dma((5,)),
            dma((5,)),
            dma((5,)),
            dma((5,)),
            dma((30,)),
            dma((40,)),
            dma((10,)),
            dma((10,)),
            dma((30,)),
            dma((30,)),
            dma((6,)),
            dma((6,)),
            dma((6,)),
            dma((6,)),
        ],
        compiler_params=pltpu.CompilerParams(
            collective_id=0, has_side_effects=True, vmem_limit_bytes=63 * 2**20
        ),
        cost_estimate=pl.CostEstimate(flops=24 * 10**9, bytes_accessed=24 * 10**6, transcendentals=10**6),
    )(tokens, expert_ids.T, gate_weights.T, w_gate, w_up, w_down)


def solution(mesh):
    in_specs = (
        P(("group", "lane"), None),
        P(("group", "lane"), None),
        P(("group", "lane"), None),
        P(("group", "lane"), None, None),
        P(("group", "lane"), None, None),
        P(("group", "lane"), None, None),
    )
    out_specs = P(("group", "lane"), None)
    return jax.shard_map(
        per_device, mesh=mesh, in_specs=in_specs, out_specs=out_specs, check_vma=False
    )
```
